512 devices in a mesh: grp: 16 (over x, z_lo), blk: 32 (over y, z_hi, core).
Axes of the slice: x: 4, y: 4, z: 16 (z_hi: 4, z_lo: 4; z = z_hi * 4 + z_lo), core: 2. Of those that a mesh axis runs over, the one named last changes fastest.
Arguments:
- points: float32 [32, 65536], P(None, ('grp', 'blk')), may hold values from -6 to 6
- length_scales: float32 [32], replicated, may hold values from 1.5 to 6
- noise_level: float32 [1], replicated, may hold values from 0.3 to 1
- targets: float32 [16, 65536], P(None, ('grp', 'blk')), may hold values from -6 to 6
Outputs:
- solution_field: float32 [16, 65536], P(None, ('grp', 'blk'))
- residual: float32 [16, 65536], P(None, ('grp', 'blk'))
The draws below stay inside these ranges and needn't reach their ends.
All inputs are finite; a program needn't handle non-finite values.
Results may differ from the reference program's by a relative error of at most 0.013.
Values may be sent and summed in bfloat16 or wider, within the bound.
No kernel may reach another device: no remote copies, remote signals or barrier semaphores. Data moves between devices by JAX's collectives and lax.ppermute only.
A program may use at most 192 MiB of HBM per device.

```python
import math
import jax
import jax.numpy as jnp
from jax import lax

FEAT = 32
RHS = 16
ITERS = 2
NPTS = 65536


def levels(stream_key, dims, cuts, low, top_value):
    loudness = 1.0
    for position, blocks in cuts:
        heights = jax.random.uniform(jax.random.fold_in(jax.random.fold_in(stream_key, 6), position), (blocks,), jnp.float32, low / len(cuts), top_value / len(cuts))
        loudness = loudness * jnp.repeat(jnp.exp(heights), dims[position] // blocks).reshape((-1,) + (1,) * (len(dims) - 1 - position))
    return loudness


def bell_draw(key, dims, scale, limit, cuts=(), kind=jnp.bfloat16):
    values = jax.random.normal(key, dims, jnp.float32) * scale
    if len(cuts) > 0:
        values = levels(key, dims, cuts, -0.22, 0.18) * values
    return jnp.clip(values, min=-limit, max=limit).astype(kind)


def setup_inputs(seed: int = 0) -> dict:
    seeds = jax.random.split(jax.random.key(seed), 5)
    points = bell_draw(seeds[0], (FEAT, NPTS), 1.0, 6.0, ((1, 512),), jnp.float32)
    length_scales = jnp.clip(jnp.exp(jax.random.uniform(seeds[1], (FEAT,), jnp.float32, math.log(1.5), math.log(6.0))), 1.5, 6.0)
    noise_level = jnp.clip(jnp.exp(jax.random.uniform(seeds[2], (1,), jnp.float32, math.log(0.3), math.log(1.0))), 0.3, 1.0)
    targets = bell_draw(seeds[3], (RHS, NPTS), 1.0, 6.0, ((1, 512),), jnp.float32)
    return dict(points=points, length_scales=length_scales, noise_level=noise_level, targets=targets)


SQRT_FIVE = math.sqrt(5.0)

def matern(dist2):
    spread = SQRT_FIVE * jnp.sqrt(jnp.maximum(dist2, 0.0))
    return ((1.0 + spread + spread * spread / 3.0) * jnp.exp(-spread)).astype(jnp.bfloat16)

def kernel_tile(rows_z, rows_sq, cols_z, cols_sq):
    inner = lax.dot_general(rows_z, cols_z, (((0,), (0,)), ((), ())), precision=lax.Precision.HIGHEST, preferred_element_type=jnp.float32)
    return matern(rows_sq[:, None] + cols_sq[None, :] - 2.0 * inner)

def apply_kernel(scaled, squares, direction, noise_value):
    total = scaled.shape[1]
    block_rows = 1024 if total % 1024 == 0 else total
    count = total // block_rows
    probes = direction.astype(jnp.bfloat16)
    row_z = jnp.moveaxis(scaled.reshape(scaled.shape[0], count, block_rows), 1, 0)
    row_sq = squares.reshape(count, block_rows)

    def one_block(pieces):
        tile = kernel_tile(pieces[0], pieces[1], scaled, squares)
        return lax.dot_general(probes, tile, (((1,), (1,)), ((), ())), preferred_element_type=jnp.float32)
    blocks = lax.map(one_block, (row_z, row_sq))
    product = jnp.transpose(blocks, (1, 0, 2)).reshape(direction.shape)
    return product + noise_value * direction

def reference(points, length_scales, noise_level, targets):
    scaled = points / length_scales[:, None]
    squares = lax.optimization_barrier(jnp.sum(scaled * scaled, axis=0))
    solution_field = jnp.zeros_like(targets)
    residual = targets
    direction = targets
    norm_now = lax.optimization_barrier(jnp.sum(residual * residual, axis=1))
    for step in range(ITERS):
        image = apply_kernel(scaled, squares, direction, noise_level[0])
        alpha = norm_now / lax.optimization_barrier(jnp.sum(direction * image, axis=1))
        solution_field = solution_field + alpha[:, None] * direction
        residual = residual - alpha[:, None] * image
        if step + 1 < ITERS:
            norm_next = lax.optimization_barrier(jnp.sum(residual * residual, axis=1))
            direction = residual + (norm_next / norm_now)[:, None] * direction
            norm_now = norm_next
    return (solution_field, residual)
```

```python
import itertools
import math

import jax
import jax.numpy as jnp
from jax import lax
from jax.experimental import pallas as pl
from jax.experimental.pallas import tpu as pltpu
from jax.sharding import PartitionSpec as P

FEAT = 32
RHS = 16
OWN = 128
ROWS = 32
COLS = 16
DEPTH = 144
TALL = 512

BOTH = ("grp", "blk")
SIZES = {"x": 4, "z_lo": 4, "y": 4, "z_hi": 4, "core": 2}
PAIRS = [[2 * i, 2 * i + 1] for i in range(16)]


def groups_along(axes):
    rest = [axis for axis in SIZES if axis not in axes]
    found = []
    for fixed in itertools.product(*[range(SIZES[axis]) for axis in rest]):
        members = []
        for moving in itertools.product(*[range(SIZES[axis]) for axis in axes]):
            place = dict(zip(rest, fixed)) | dict(zip(axes, moving))
            index = 0
            for axis in SIZES:
                index = index * SIZES[axis] + place[axis]
            members.append(index)
        found.append(members)
    return found


ALONG_Z = groups_along(["z_hi", "z_lo"])
IN_PLANE = groups_along(["x", "y"])


def exchange(pieces, groups):
    return lax.all_to_all(pieces, BOTH, 0, 0, axis_index_groups=groups)


def spread(value, groups):
    return exchange(jnp.broadcast_to(value[None], (16,) + value.shape), groups)


def from_rows(value):
    column = spread(value, ALONG_Z)
    return lax.all_gather(column, "blk", axis_index_groups=PAIRS, axis=0, tiled=True)


def parts(value, count):
    found = []
    for _ in range(count):
        part = value.astype(jnp.bfloat16)
        found.append(part)
        value = value - part.astype(jnp.float32)
    return found


def operand(scaled, scale, left):
    squares = 5.0 * jnp.sum(scaled * scaled, axis=0, keepdims=True)
    high, low = parts(scaled * scale, 2)
    pieces = parts(squares, 3)
    ones = [jnp.ones_like(pieces[0])] * 3
    rest = jnp.zeros((DEPTH - 4 * FEAT - 6, scaled.shape[1]), jnp.bfloat16)
    if left:
        rows = [high, low, high, low] + pieces + ones
    else:
        rows = [high, high, low, low] + ones + pieces
    return jnp.concatenate(rows + [rest], axis=0)


def matern(five_dist2):
    five_dist2 = jnp.maximum(five_dist2, 1e-30)
    spread_ = five_dist2 * lax.rsqrt(five_dist2)
    decay = jnp.exp2(spread_ * (-math.log2(math.e)))
    return ((spread_ + 1.0) + five_dist2 * (1.0 / 3.0)) * decay


def build_kernel(rows_ref, cols_ref, tile_ref, product_ref, right, total):
    for block in range(COLS):
        right[:, block * OWN : (block + 1) * OWN] = operand(cols_ref[block], -10.0, False)
    total[...] = jnp.zeros_like(total)
    count = TALL // OWN

    def step(index, carry):
        blocks = [rows_ref[index * count + i] for i in range(count)]
        scaled = jnp.concatenate([block[:FEAT] for block in blocks], axis=1)
        probes = jnp.concatenate([block[FEAT:] for block in blocks], axis=1)
        probes = jnp.concatenate(parts(probes, 2), axis=0)
        left = operand(scaled, 1.0, True)
        dist = lax.dot_general(
            left, right[...], (((0,), (0,)), ((), ())), preferred_element_type=jnp.float32
        )
        kernel = matern(dist).astype(jnp.bfloat16)
        tile_ref[pl.ds(pl.multiple_of(index * TALL, TALL), TALL), :] = kernel
        total[...] += jnp.dot(probes, kernel, preferred_element_type=jnp.float32)
        return carry

    lax.fori_loop(0, ROWS // count, step, 0)
    put_product(total[...], product_ref)


def put_product(total, product_ref):
    both = total[:RHS] + total[RHS:]
    for block in range(COLS):
        product_ref[block] = both[:, block * OWN : (block + 1) * OWN]


def build(rows, cols):
    return pl.pallas_call(
        build_kernel,
        out_shape=(
            pltpu.VMEM((ROWS * OWN, COLS * OWN), jnp.bfloat16),
            jax.ShapeDtypeStruct((COLS, RHS, OWN), jnp.float32),
        ),
        in_specs=[pl.BlockSpec(memory_space=pltpu.VMEM)] * 2,
        out_specs=(pl.BlockSpec(memory_space=pltpu.VMEM),) * 2,
        scratch_shapes=[
            pltpu.VMEM((DEPTH, COLS * OWN), jnp.bfloat16),
            pltpu.VMEM((2 * RHS, COLS * OWN), jnp.float32),
        ],
        compiler_params=pltpu.CompilerParams(vmem_limit_bytes=24 * 2**20),
        name="build",
    )(rows, cols)


def again_kernel(probes_ref, tile_ref, product_ref):
    probes = jnp.concatenate([probes_ref[i] for i in range(ROWS)], axis=1)
    probes = jnp.concatenate(parts(probes, 2), axis=0)
    put_product(jnp.dot(probes, tile_ref[...], preferred_element_type=jnp.float32), product_ref)


def again(probes, tile):
    return pl.pallas_call(
        again_kernel,
        out_shape=jax.ShapeDtypeStruct((COLS, RHS, OWN), jnp.float32),
        in_specs=[pl.BlockSpec(memory_space=pltpu.VMEM)] * 2,
        out_specs=pl.BlockSpec(memory_space=pltpu.VMEM),
        compiler_params=pltpu.CompilerParams(vmem_limit_bytes=24 * 2**20),
        name="again",
    )(probes, tile)


def own_sum(partials):
    return jnp.sum(exchange(partials, IN_PLANE), axis=0)


def on_device(points, length_scales, noise_level, targets):
    scaled = (points / length_scales[:, None]).astype(jnp.float16)
    sent = jnp.concatenate([scaled, targets.astype(jnp.float16)], axis=0)
    cols = spread(scaled, IN_PLANE).astype(jnp.float32)
    rows = from_rows(sent).astype(jnp.float32)

    noise = noise_level[0]
    tile, partials = build(rows, cols)
    first = own_sum(partials) + noise * targets
    second = own_sum(again(from_rows(first), tile)) + noise * first

    pairs = [
        targets * targets,
        targets * first,
        first * first,
        targets * second,
        first * second,
    ]
    own = jnp.stack([jnp.sum(pair, axis=1) for pair in pairs]).reshape(1, -1)
    own = jnp.pad(own, ((0, 0), (0, OWN - own.shape[1])))
    near = jnp.sum(spread(own, IN_PLANE), axis=0)
    sums = jnp.sum(from_rows(near), axis=0)[0, : 5 * RHS].reshape(5, RHS)
    norm, curve, square, cross, cubic = sums
    alpha = norm / curve
    norm_next = norm - 2.0 * alpha * curve + alpha * alpha * square
    ratio = norm_next / norm
    keep = 1.0 + ratio
    curve_next = keep * keep * curve - keep * alpha * (square + cross) + alpha * alpha * cubic
    alpha_next = norm_next / curve_next
    alpha, keep, alpha_next = alpha[:, None], keep[:, None], alpha_next[:, None]
    direction = keep * targets - alpha * first
    image = keep * first - alpha * second
    solution_field = alpha * targets + alpha_next * direction
    residual = (targets - alpha * first) - alpha_next * image
    return (solution_field, residual)


def solution(mesh):
    return jax.shard_map(
        on_device,
        mesh=mesh,
        in_specs=(P(None, BOTH), P(), P(), P(None, BOTH)),
        out_specs=(P(None, BOTH), P(None, BOTH)),
        check_vma=False,
    )
```

```python
import itertools
import math

import jax
import jax.numpy as jnp
from jax import lax
from jax.experimental import pallas as pl
from jax.experimental.pallas import tpu as pltpu
from jax.sharding import PartitionSpec as P

FEAT = 32
RHS = 16
OWN = 128
ROWS = 32
COLS = 16
DEPTH = 144
WIDE = 256
CHUNKS = COLS * OWN // WIDE

BOTH = ("grp", "blk")
SIZES = {"x": 4, "z_lo": 4, "y": 4, "z_hi": 4, "core": 2}
PAIRS = [[2 * i, 2 * i + 1] for i in range(16)]


def groups_along(axes):
    rest = [axis for axis in SIZES if axis not in axes]
    found = []
    for fixed in itertools.product(*[range(SIZES[axis]) for axis in rest]):
        members = []
        for moving in itertools.product(*[range(SIZES[axis]) for axis in axes]):
            place = dict(zip(rest, fixed)) | dict(zip(axes, moving))
            index = 0
            for axis in SIZES:
                index = index * SIZES[axis] + place[axis]
            members.append(index)
        found.append(members)
    return found


ALONG_Z = groups_along(["z_hi", "z_lo"])
IN_PLANE = groups_along(["y", "x"])


def exchange(pieces, groups):
    return lax.all_to_all(pieces, BOTH, 0, 0, axis_index_groups=groups)


def spread(value, groups):
    return exchange(jnp.broadcast_to(value[None], (16,) + value.shape), groups)


def from_rows(value):
    column = spread(value, ALONG_Z)
    return lax.all_gather(column, "blk", axis_index_groups=PAIRS, axis=0, tiled=True)


def parts(value, count):
    found = []
    for _ in range(count):
        part = value.astype(jnp.bfloat16)
        found.append(part)
        value = value - part.astype(jnp.float32)
    return found


def operand(scaled, scale, left):
    squares = 5.0 * jnp.sum(scaled * scaled, axis=0, keepdims=True)
    high, low = parts(scaled * scale, 2)
    pieces = parts(squares, 3)
    ones = [jnp.ones_like(pieces[0])] * 3
    rest = jnp.zeros((DEPTH - 4 * FEAT - 6, scaled.shape[1]), jnp.bfloat16)
    if left:
        rows = [high, low, high, low] + pieces + ones
    else:
        rows = [high, high, low, low] + ones + pieces
    return jnp.concatenate(rows + [rest], axis=0)


def matern(five_dist2):
    five_dist2 = jnp.maximum(five_dist2, 1e-30)
    spread_ = five_dist2 * lax.rsqrt(five_dist2)
    decay = jnp.exp2(spread_ * (-math.log2(math.e)))
    return ((spread_ + 1.0) + five_dist2 * (1.0 / 3.0)) * decay


def put_product(total, chunk, product_ref):
    both = total[:RHS] + total[RHS:]
    for block in range(WIDE // OWN):
        product_ref[chunk * (WIDE // OWN) + block] = both[:, block * OWN : (block + 1) * OWN]


def stacked(pieces):
    return jnp.concatenate(parts(jnp.concatenate(pieces, axis=1), 2), axis=0)


def build_kernel(rows_ref, cols_ref, tile_ref, product_ref, left, right, probes, held, sems):
    for block in range(COLS):
        right[:, block * OWN : (block + 1) * OWN] = operand(cols_ref[block], -10.0, False)
    for some in range(0, ROWS, 4):
        blocks = [rows_ref[some + i] for i in range(4)]
        at = slice(some * OWN, (some + 4) * OWN)
        scaled = jnp.concatenate([block[:FEAT] for block in blocks], axis=1)
        left[at, :] = operand(scaled, 1.0, True).T
        probes[:, at] = stacked([block[FEAT:] for block in blocks])

    def leave(chunk):
        slot = chunk % 2
        return pltpu.make_async_copy(held.at[slot], tile_ref.at[chunk], sems.at[slot])

    def step(chunk, carry):
        @pl.when(chunk >= 2)
        def _():
            leave(chunk - 2).wait()

        cols = pl.ds(pl.multiple_of(chunk * WIDE, WIDE), WIDE)
        dist = jnp.dot(left[...], right[:, cols], preferred_element_type=jnp.float32)
        kernel = matern(dist).astype(jnp.bfloat16)
        held[chunk % 2] = kernel
        total = jnp.dot(probes[...], kernel, preferred_element_type=jnp.float32)
        put_product(total, chunk, product_ref)
        leave(chunk).start()
        return carry

    lax.fori_loop(0, CHUNKS, step, 0)
    leave(CHUNKS - 2).wait()
    leave(CHUNKS - 1).wait()


def build(rows, cols):
    return pl.pallas_call(
        build_kernel,
        out_shape=(
            jax.ShapeDtypeStruct((CHUNKS, ROWS * OWN, WIDE), jnp.bfloat16),
            jax.ShapeDtypeStruct((COLS, RHS, OWN), jnp.float32),
        ),
        in_specs=[pl.BlockSpec(memory_space=pltpu.VMEM)] * 2,
        out_specs=(pl.BlockSpec(memory_space=pl.ANY), pl.BlockSpec(memory_space=pltpu.VMEM)),
        scratch_shapes=[
            pltpu.VMEM((ROWS * OWN, DEPTH), jnp.bfloat16),
            pltpu.VMEM((DEPTH, COLS * OWN), jnp.bfloat16),
            pltpu.VMEM((2 * RHS, ROWS * OWN), jnp.bfloat16),
            pltpu.VMEM((2, ROWS * OWN, WIDE), jnp.bfloat16),
            pltpu.SemaphoreType.DMA((2,)),
        ],
        compiler_params=pltpu.CompilerParams(vmem_limit_bytes=40 * 2**20),
        name="build",
    )(rows, cols)


def again_kernel(probes_ref, tile_ref, product_ref, held, sems):
    def fetch(chunk):
        return pltpu.make_async_copy(tile_ref.at[chunk], held.at[chunk], sems.at[chunk])

    for chunk in range(CHUNKS):
        fetch(chunk).start()
    probes = stacked([probes_ref[i] for i in range(ROWS)])
    for chunk in range(CHUNKS):
        fetch(chunk).wait()
        total = jnp.dot(probes, held[chunk], preferred_element_type=jnp.float32)
        put_product(total, chunk, product_ref)


def again(probes, tile):
    return pl.pallas_call(
        again_kernel,
        out_shape=jax.ShapeDtypeStruct((COLS, RHS, OWN), jnp.float32),
        in_specs=[pl.BlockSpec(memory_space=pltpu.VMEM), pl.BlockSpec(memory_space=pl.ANY)],
        out_specs=pl.BlockSpec(memory_space=pltpu.VMEM),
        scratch_shapes=[
            pltpu.VMEM((CHUNKS, ROWS * OWN, WIDE), jnp.bfloat16),
            pltpu.SemaphoreType.DMA((CHUNKS,)),
        ],
        compiler_params=pltpu.CompilerParams(vmem_limit_bytes=40 * 2**20),
        name="again",
    )(probes, tile)


def own_sum(partials):
    return jnp.sum(exchange(partials, IN_PLANE), axis=0)


def on_device(points, length_scales, noise_level, targets):
    scaled = (points / length_scales[:, None]).astype(jnp.float16)
    sent = jnp.concatenate([scaled, targets.astype(jnp.float16)], axis=0)
    cols = spread(scaled, IN_PLANE).astype(jnp.float32)
    rows = from_rows(sent).astype(jnp.float32)

    noise = noise_level[0]
    tile, partials = build(rows, cols)
    first = own_sum(partials) + noise * targets
    second = own_sum(again(from_rows(first), tile)) + noise * first

    pairs = [
        targets * targets,
        targets * first,
        first * first,
        targets * second,
        first * second,
    ]
    own = jnp.stack([jnp.sum(pair, axis=1) for pair in pairs]).reshape(1, -1)
    own = jnp.pad(own, ((0, 0), (0, OWN - own.shape[1])))
    near = jnp.sum(spread(own, IN_PLANE), axis=0)
    sums = jnp.sum(from_rows(near), axis=0)[0, : 5 * RHS].reshape(5, RHS)
    norm, curve, square, cross, cubic = sums
    alpha = norm / curve
    norm_next = norm - 2.0 * alpha * curve + alpha * alpha * square
    ratio = norm_next / norm
    keep = 1.0 + ratio
    curve_next = keep * keep * curve - keep * alpha * (square + cross) + alpha * alpha * cubic
    alpha_next = norm_next / curve_next
    alpha, keep, alpha_next = alpha[:, None], keep[:, None], alpha_next[:, None]
    direction = keep * targets - alpha * first
    image = keep * first - alpha * second
    solution_field = alpha * targets + alpha_next * direction
    residual = (targets - alpha * first) - alpha_next * image
    return (solution_field, residual)


def solution(mesh):
    return jax.shard_map(
        on_device,
        mesh=mesh,
        in_specs=(P(None, BOTH), P(), P(), P(None, BOTH)),
        out_specs=(P(None, BOTH), P(None, BOTH)),
        check_vma=False,
    )
```

```python
import itertools
import math

import jax
import jax.numpy as jnp
from jax import lax
from jax.experimental import pallas as pl
from jax.experimental.pallas import tpu as pltpu
from jax.sharding import PartitionSpec as P

FEAT = 32
RHS = 16
OWN = 128
ROWS = 32
COLS = 16
DEPTH = 144
WIDE = 256
CHUNKS = COLS * OWN // WIDE

BOTH = ("grp", "blk")
SIZES = {"x": 4, "z_lo": 4, "y": 4, "z_hi": 4, "core": 2}
PAIRS = [[2 * i, 2 * i + 1] for i in range(16)]


def groups_along(axes):
    rest = [axis for axis in SIZES if axis not in axes]
    found = []
    for fixed in itertools.product(*[range(SIZES[axis]) for axis in rest]):
        members = []
        for moving in itertools.product(*[range(SIZES[axis]) for axis in axes]):
            place = dict(zip(rest, fixed)) | dict(zip(axes, moving))
            index = 0
            for axis in SIZES:
                index = index * SIZES[axis] + place[axis]
            members.append(index)
        found.append(members)
    return found


ALONG_Z = groups_along(["z_hi", "z_lo"])
IN_PLANE = groups_along(["y", "x"])
IN_PLANE_PAIR = groups_along(["y", "x", "core"])


def exchange(pieces, groups):
    return lax.all_to_all(pieces, BOTH, 0, 0, axis_index_groups=groups)


def copies(value, groups):
    return jnp.broadcast_to(value[None], (len(groups[0]),) + value.shape)


def spread(value, groups):
    return exchange(copies(value, groups), groups)


def from_pair(value):
    return lax.all_gather(value, "blk", axis_index_groups=PAIRS, axis=0, tiled=True)


def pressed(value, power, scale):
    size = jnp.exp2(jnp.log2(jnp.abs(value)) * (1.0 / power)) * scale
    return jnp.where(value < 0.0, -size, size).astype(jnp.float16)


def unpressed(value, power, scale):
    root = value.astype(jnp.float32) * (1.0 / scale)
    return root * jnp.abs(root) if power == 2 else root * root * root


def parts(value, count):
    found = []
    for _ in range(count):
        part = value.astype(jnp.bfloat16)
        found.append(part)
        value = value - part.astype(jnp.float32)
    return found


def operand(scaled, scale, left):
    squares = 5.0 * jnp.sum(scaled * scaled, axis=0, keepdims=True)
    high, low = parts(scaled * scale, 2)
    pieces = parts(squares, 3)
    ones = [jnp.ones_like(pieces[0])] * 3
    rest = jnp.zeros((DEPTH - 4 * FEAT - 6, scaled.shape[1]), jnp.bfloat16)
    if left:
        rows = [high, low, high, low] + pieces + ones
    else:
        rows = [high, high, low, low] + ones + pieces
    return jnp.concatenate(rows + [rest], axis=0)


def matern(five_dist2):
    five_dist2 = jnp.maximum(five_dist2, 1e-30)
    spread_ = five_dist2 * lax.rsqrt(five_dist2)
    decay = jnp.exp2(spread_ * (-math.log2(math.e)))
    return ((spread_ + 1.0) + five_dist2 * (1.0 / 3.0)) * decay


def put_product(total, chunk, product_ref):
    both = total[:RHS] + total[RHS:]
    for block in range(WIDE // OWN):
        product_ref[chunk * (WIDE // OWN) + block] = both[:, block * OWN : (block + 1) * OWN]


def stacked(pieces):
    return jnp.concatenate(parts(jnp.concatenate(pieces, axis=1), 2), axis=0)


def build_kernel(rows_ref, cols_ref, tile_ref, product_ref, left, right, probes, even, odd, sems):
    held = [even, odd]
    for block in range(COLS):
        right[:, block * OWN : (block + 1) * OWN] = operand(cols_ref[block], -10.0, False)
    for some in range(0, ROWS, 4):
        blocks = [rows_ref[some + i] for i in range(4)]
        at = slice(some * OWN, (some + 4) * OWN)
        scaled = jnp.concatenate([block[:FEAT] for block in blocks], axis=1)
        left[at, :] = operand(scaled, 1.0, True).T
        probes[:, at] = stacked([block[FEAT:] for block in blocks])

    def leave(chunk, slot):
        return pltpu.make_async_copy(held[slot], tile_ref.at[chunk], sems.at[slot])

    def step(pair, carry):
        for slot in range(2):
            chunk = 2 * pair + slot

            @pl.when(pair >= 1)
            def _():
                leave(chunk - 2, slot).wait()

            cols = pl.ds(pl.multiple_of(chunk * WIDE, WIDE), WIDE)
            dist = jnp.dot(left[...], right[:, cols], preferred_element_type=jnp.float32)
            held[slot][...] = matern(dist).astype(jnp.bfloat16)
            total = jnp.dot(probes[...], held[slot][...], preferred_element_type=jnp.float32)
            put_product(total, chunk, product_ref)
            leave(chunk, slot).start()
        return carry

    lax.fori_loop(0, CHUNKS // 2, step, 0)
    for slot in range(2):
        leave(CHUNKS - 2 + slot, slot).wait()


def build(rows, cols):
    return pl.pallas_call(
        build_kernel,
        out_shape=(
            jax.ShapeDtypeStruct((CHUNKS, ROWS * OWN, WIDE), jnp.bfloat16),
            jax.ShapeDtypeStruct((COLS, RHS, OWN), jnp.float32),
        ),
        in_specs=[pl.BlockSpec(memory_space=pltpu.VMEM)] * 2,
        out_specs=(pl.BlockSpec(memory_space=pl.ANY), pl.BlockSpec(memory_space=pltpu.VMEM)),
        scratch_shapes=[
            pltpu.VMEM((ROWS * OWN, DEPTH), jnp.bfloat16),
            pltpu.VMEM((DEPTH, COLS * OWN), jnp.bfloat16),
            pltpu.VMEM((2 * RHS, ROWS * OWN), jnp.bfloat16),
            pltpu.VMEM((ROWS * OWN, WIDE), jnp.bfloat16),
            pltpu.VMEM((ROWS * OWN, WIDE), jnp.bfloat16),
            pltpu.SemaphoreType.DMA((2,)),
        ],
        compiler_params=pltpu.CompilerParams(vmem_limit_bytes=40 * 2**20),
        name="build",
    )(rows, cols)


def again_kernel(probes_ref, tile_ref, product_ref, held, sems):
    def fetch(chunk):
        return pltpu.make_async_copy(tile_ref.at[chunk], held.at[chunk], sems.at[chunk])

    for chunk in range(CHUNKS):
        fetch(chunk).start()
    probes = stacked([probes_ref[i] for i in range(ROWS)])
    for chunk in range(CHUNKS):
        fetch(chunk).wait()
        total = jnp.dot(probes, held[chunk], preferred_element_type=jnp.float32)
        put_product(total, chunk, product_ref)


def again(probes, tile):
    return pl.pallas_call(
        again_kernel,
        out_shape=jax.ShapeDtypeStruct((COLS, RHS, OWN), jnp.float32),
        in_specs=[pl.BlockSpec(memory_space=pltpu.VMEM), pl.BlockSpec(memory_space=pl.ANY)],
        out_specs=pl.BlockSpec(memory_space=pltpu.VMEM),
        scratch_shapes=[
            pltpu.VMEM((CHUNKS, ROWS * OWN, WIDE), jnp.bfloat16),
            pltpu.SemaphoreType.DMA((CHUNKS,)),
        ],
        compiler_params=pltpu.CompilerParams(vmem_limit_bytes=40 * 2**20),
        name="again",
    )(probes, tile)


def own_sum(partials):
    return jnp.sum(exchange(partials, IN_PLANE), axis=0)


def on_device(points, length_scales, noise_level, targets):
    scaled = (points / length_scales[:, None]).astype(jnp.float16)
    sent = jnp.concatenate([scaled, pressed(targets, 2, 2.0**14)], axis=0)
    column = spread(sent, ALONG_Z)
    ready, column = lax.optimization_barrier((copies(scaled, IN_PLANE), column))
    cols = exchange(ready, IN_PLANE).astype(jnp.float32)
    rows = from_pair(column)
    rows = jnp.concatenate(
        [rows[:, :FEAT].astype(jnp.float32), unpressed(rows[:, FEAT:], 2, 2.0**14)], axis=1
    )

    noise = noise_level[0]
    tile, partials = build(rows, cols)
    first = own_sum(partials) + noise * targets
    probes = unpressed(from_pair(spread(pressed(first, 3, 2.0**9), ALONG_Z)), 3, 2.0**9)
    second = own_sum(again(probes, tile)) + noise * first

    pairs = [
        targets * targets,
        targets * first,
        first * first,
        targets * second,
        first * second,
    ]
    own = jnp.stack([jnp.sum(pair, axis=1) for pair in pairs]).reshape(1, -1)
    own = jnp.pad(own, ((0, 0), (0, OWN - own.shape[1])))
    near = jnp.sum(spread(own, IN_PLANE_PAIR), axis=0)
    sums = jnp.sum(spread(near, ALONG_Z), axis=0)[0, : 5 * RHS].reshape(5, RHS)
    norm, curve, square, cross, cubic = sums
    alpha = norm / curve
    norm_next = norm - 2.0 * alpha * curve + alpha * alpha * square
    ratio = norm_next / norm
    keep = 1.0 + ratio
    curve_next = keep * keep * curve - keep * alpha * (square + cross) + alpha * alpha * cubic
    alpha_next = norm_next / curve_next
    alpha, keep, alpha_next = alpha[:, None], keep[:, None], alpha_next[:, None]
    direction = keep * targets - alpha * first
    image = keep * first - alpha * second
    solution_field = alpha * targets + alpha_next * direction
    residual = (targets - alpha * first) - alpha_next * image
    return (solution_field, residual)


def solution(mesh):
    return jax.shard_map(
        on_device,
        mesh=mesh,
        in_specs=(P(None, BOTH), P(), P(), P(None, BOTH)),
        out_specs=(P(None, BOTH), P(None, BOTH)),
        check_vma=False,
    )
```

```python
import itertools
import math

import jax
import jax.numpy as jnp
from jax import lax
from jax.experimental import pallas as pl
from jax.experimental.pallas import tpu as pltpu
from jax.sharding import PartitionSpec as P

FEAT = 32
RHS = 16
OWN = 128
ROWS = 32
COLS = 16
DEPTH = 144
WIDE = 256
CHUNKS = COLS * OWN // WIDE
STEPS = 29.9
SQRT_FIVE = math.sqrt(5.0)
HELD = 4

BOTH = ("grp", "blk")
SIZES = {"x": 4, "z_lo": 4, "y": 4, "z_hi": 4, "core": 2}
PAIRS = [[2 * i, 2 * i + 1] for i in range(16)]


def groups_along(axes):
    rest = [axis for axis in SIZES if axis not in axes]
    found = []
    for fixed in itertools.product(*[range(SIZES[axis]) for axis in rest]):
        members = []
        for moving in itertools.product(*[range(SIZES[axis]) for axis in axes]):
            place = dict(zip(rest, fixed)) | dict(zip(axes, moving))
            index = 0
            for axis in SIZES:
                index = index * SIZES[axis] + place[axis]
            members.append(index)
        found.append(members)
    return found


ALONG_Z = groups_along(["z_hi", "z_lo"])
IN_PLANE = groups_along(["y", "x"])
IN_PLANE_PAIR = groups_along(["y", "x", "core"])


def exchange(pieces, groups):
    return lax.all_to_all(pieces, BOTH, 0, 0, axis_index_groups=groups)


def copies(value, groups):
    return jnp.broadcast_to(value[None], (len(groups[0]),) + value.shape)


def spread(value, groups):
    return exchange(copies(value, groups), groups)


def from_pair(value):
    return lax.all_gather(value, "blk", axis_index_groups=PAIRS, axis=0, tiled=True)


def even_code(points):
    size = jnp.abs(points) * (STEPS / 6.0)
    whole = jnp.floor(size)
    code = jnp.exp2(whole - 14.0) * (1.0 + (size - whole))
    return jnp.where(points < 0.0, -code, code).astype(jnp.float16)


def even_points(code):
    code = code.astype(jnp.float32)
    whole = jnp.floor(jnp.log2(jnp.abs(code)))
    size = (whole + 13.0 + jnp.abs(code) * jnp.exp2(-whole)) * (6.0 / STEPS)
    return jnp.where(code < 0.0, -size, size)


def two_codes(values):
    high = (values.astype(jnp.bfloat16).astype(jnp.float32) * 2.0**13).astype(jnp.float16)
    low = (values - high.astype(jnp.float32) * 2.0**-13) * 2.0**21
    return [high, low.astype(jnp.float16)]


def from_two_codes(high, low):
    return high.astype(jnp.float32) * 2.0**-13 + low.astype(jnp.float32) * 2.0**-21


def parts(value, count):
    found = []
    for _ in range(count):
        part = value.astype(jnp.bfloat16)
        found.append(part)
        value = value - part.astype(jnp.float32)
    return found


def operand(coords, left):
    high, low = parts(coords, 2)
    kept = high.astype(jnp.float32) + low.astype(jnp.float32)
    pieces = parts(jnp.sum(kept * kept, axis=0, keepdims=True), 3)
    ones = [jnp.ones_like(pieces[0])] * 3
    rest = jnp.zeros((DEPTH - 4 * FEAT - 6, coords.shape[1]), jnp.bfloat16)
    if left:
        rows = [high, low, high, low] + pieces + ones
    else:
        high, low = high * -2.0, low * -2.0
        rows = [high, high, low, low] + ones + pieces
    return jnp.concatenate(rows + [rest], axis=0)


def matern(five_dist2):
    five_dist2 = jnp.maximum(five_dist2, 1e-30)
    spread_ = five_dist2 * lax.rsqrt(five_dist2)
    decay = jnp.exp2(spread_ * (-math.log2(math.e)))
    return ((spread_ + 1.0) + five_dist2 * (1.0 / 3.0)) * decay


def ready_kernel(
    points_ref, scales_ref, noise_ref, targets_ref,
    points_out_ref, targets_out_ref, scales_out_ref, noise_out_ref,
):
    points_out_ref[...] = points_ref[...]
    targets_out_ref[...] = targets_ref[...]
    scales_out_ref[...] = jnp.broadcast_to(scales_ref[...].reshape(1, FEAT), (OWN, FEAT)).T
    noise_out_ref[...] = jnp.full((RHS, OWN), noise_ref[0], jnp.float32)


def make_ready(points, length_scales, noise_level, targets):
    vmem = pl.BlockSpec(memory_space=pltpu.VMEM)
    return pl.pallas_call(
        ready_kernel,
        out_shape=(
            pltpu.VMEM((FEAT, OWN), jnp.float32),
            pltpu.VMEM((RHS, OWN), jnp.float32),
            pltpu.VMEM((FEAT, OWN), jnp.float32),
            pltpu.VMEM((RHS, OWN), jnp.float32),
        ),
        in_specs=[vmem, vmem, pl.BlockSpec(memory_space=pltpu.SMEM), vmem],
        out_specs=(vmem, vmem, vmem, vmem),
        name="ready",
    )(points, length_scales, noise_level, targets)


def put_product(total, chunk, product_ref):
    for block in range(WIDE // OWN):
        product_ref[chunk * (WIDE // OWN) + block] = total[:, block * OWN : (block + 1) * OWN]


def probes_of(pieces):
    return jnp.concatenate([piece.astype(jnp.bfloat16) for piece in pieces], axis=1)


def build_kernel(rows_ref, cols_ref, tile_ref, product_ref, left, right, probes, sems, *held):
    for block in range(COLS):
        right[:, block * OWN : (block + 1) * OWN] = operand(cols_ref[block], False)
    for some in range(0, ROWS, 4):
        blocks = [rows_ref[some + i] for i in range(4)]
        at = slice(some * OWN, (some + 4) * OWN)
        scaled = jnp.concatenate([block[:FEAT] for block in blocks], axis=1)
        left[at, :] = operand(scaled, True).T
        probes[:, at] = probes_of([block[FEAT:] for block in blocks])

    def leave(chunk):
        return pltpu.make_async_copy(held[chunk % HELD], tile_ref.at[chunk], sems.at[chunk % HELD])

    def multiply(chunk):
        kernel = held[chunk % HELD][...]
        total = jnp.dot(probes[...], kernel, preferred_element_type=jnp.float32)
        put_product(total, chunk, product_ref)

    for chunk in range(CHUNKS):
        if chunk >= HELD:
            leave(chunk - HELD).wait()
        cols = slice(chunk * WIDE, (chunk + 1) * WIDE)
        dist = jnp.dot(left[...], right[:, cols], preferred_element_type=jnp.float32)
        held[chunk % HELD][...] = matern(dist).astype(jnp.bfloat16)
        if chunk >= 1:
            multiply(chunk - 1)
        leave(chunk).start()
    multiply(CHUNKS - 1)
    for chunk in range(CHUNKS - HELD, CHUNKS):
        leave(chunk).wait()


def build(rows, cols):
    return pl.pallas_call(
        build_kernel,
        out_shape=(
            jax.ShapeDtypeStruct((CHUNKS, ROWS * OWN, WIDE), jnp.bfloat16),
            jax.ShapeDtypeStruct((COLS, RHS, OWN), jnp.float32),
        ),
        in_specs=[pl.BlockSpec(memory_space=pltpu.VMEM)] * 2,
        out_specs=(pl.BlockSpec(memory_space=pl.ANY), pl.BlockSpec(memory_space=pltpu.VMEM)),
        scratch_shapes=[
            pltpu.VMEM((ROWS * OWN, DEPTH), jnp.bfloat16),
            pltpu.VMEM((DEPTH, COLS * OWN), jnp.bfloat16),
            pltpu.VMEM((RHS, ROWS * OWN), jnp.bfloat16),
            pltpu.SemaphoreType.DMA((HELD,)),
            *[pltpu.VMEM((ROWS * OWN, WIDE), jnp.bfloat16) for _ in range(HELD)],
        ],
        compiler_params=pltpu.CompilerParams(vmem_limit_bytes=40 * 2**20),
        name="build",
    )(rows, cols)


def again_kernel(probes_ref, tile_ref, product_ref, held, sems):
    def fetch(chunk):
        return pltpu.make_async_copy(tile_ref.at[chunk], held.at[chunk], sems.at[chunk])

    for chunk in range(CHUNKS):
        fetch(chunk).start()
    probes = probes_of([probes_ref[i] for i in range(ROWS)])
    for chunk in range(CHUNKS):
        fetch(chunk).wait()
        total = jnp.dot(probes, held[chunk], preferred_element_type=jnp.float32)
        put_product(total, chunk, product_ref)


def again(probes, tile):
    return pl.pallas_call(
        again_kernel,
        out_shape=jax.ShapeDtypeStruct((COLS, RHS, OWN), jnp.float32),
        in_specs=[pl.BlockSpec(memory_space=pltpu.VMEM), pl.BlockSpec(memory_space=pl.ANY)],
        out_specs=pl.BlockSpec(memory_space=pltpu.VMEM),
        scratch_shapes=[
            pltpu.VMEM((CHUNKS, ROWS * OWN, WIDE), jnp.bfloat16),
            pltpu.SemaphoreType.DMA((CHUNKS,)),
        ],
        compiler_params=pltpu.CompilerParams(vmem_limit_bytes=40 * 2**20),
        name="again",
    )(probes, tile)


def own_sum(partials):
    return jnp.sum(exchange(partials, IN_PLANE), axis=0)


def as_row(sums):
    flat = jnp.stack(sums).reshape(1, -1)
    return jnp.pad(flat, ((0, 0), (0, OWN - flat.shape[1])))


def on_device(points, length_scales, noise_level, targets):
    points, targets, scales, noise = make_ready(points, length_scales, noise_level, targets)
    code = even_code(points)
    column = from_pair(spread(jnp.concatenate([code] + two_codes(targets), axis=0), ALONG_Z))
    row_coords = even_points(column[:, :FEAT]) / scales * SQRT_FIVE
    row_targets = from_two_codes(column[:, FEAT : FEAT + RHS], column[:, FEAT + RHS :])
    rows = jnp.concatenate([row_coords, row_targets], axis=1)
    code, rows = lax.optimization_barrier((code, rows))
    cols = even_points(spread(code, IN_PLANE)) / scales * SQRT_FIVE
    row_targets = rows[:, FEAT:]

    tile, partials = build(rows, cols)
    image = own_sum(partials) + noise * targets
    row_image = from_pair(spread(image, ALONG_Z))

    norm = jnp.sum(row_targets * row_targets, axis=(0, 2))
    curve = jnp.sum(row_targets * row_image, axis=(0, 2))
    square = jnp.sum(row_image * row_image, axis=(0, 2))
    sums = jnp.sum(spread(as_row([norm, curve, square]), IN_PLANE), axis=0)
    norm, curve, square = sums[0, : 3 * RHS].reshape(3, RHS)
    alpha = norm / curve
    norm_next = norm - 2.0 * alpha * curve + alpha * alpha * square
    ratio = (norm_next / norm)[:, None]
    alpha = alpha[:, None]

    row_direction = (row_targets - alpha * row_image) + ratio * row_targets
    partials = again(row_direction, tile)
    residual = targets - alpha * image
    direction = residual + ratio * targets
    image_next = own_sum(partials) + noise * direction
    near = jnp.sum(spread(as_row([jnp.sum(direction * image_next, axis=1)]), IN_PLANE_PAIR), axis=0)
    curve_next = jnp.sum(spread(near, ALONG_Z), axis=0)[0, :RHS]
    alpha_next = (norm_next / curve_next)[:, None]
    solution_field = alpha * targets + alpha_next * direction
    residual = residual - alpha_next * image_next
    return (solution_field, residual)


def solution(mesh):
    return jax.shard_map(
        on_device,
        mesh=mesh,
        in_specs=(P(None, BOTH), P(), P(), P(None, BOTH)),
        out_specs=(P(None, BOTH), P(None, BOTH)),
        check_vma=False,
    )
```

```python
import itertools
import math

import jax
import jax.numpy as jnp
from jax import lax
from jax.experimental import pallas as pl
from jax.experimental.pallas import tpu as pltpu
from jax.sharding import PartitionSpec as P

FEAT = 32
RHS = 16
OWN = 128
ROWS = 32
COLS = 16
DEPTH = 144
WIDE = 256
CHUNKS = COLS * OWN // WIDE
STEPS = 29.9
SQRT_FIVE = math.sqrt(5.0)
HELD = 4

BOTH = ("grp", "blk")
SIZES = {"x": 4, "z_lo": 4, "y": 4, "z_hi": 4, "core": 2}
PAIRS = [[2 * i, 2 * i + 1] for i in range(16)]


def groups_along(axes):
    rest = [axis for axis in SIZES if axis not in axes]
    found = []
    for fixed in itertools.product(*[range(SIZES[axis]) for axis in rest]):
        members = []
        for moving in itertools.product(*[range(SIZES[axis]) for axis in axes]):
            place = dict(zip(rest, fixed)) | dict(zip(axes, moving))
            index = 0
            for axis in SIZES:
                index = index * SIZES[axis] + place[axis]
            members.append(index)
        found.append(members)
    return found


ALONG_Z = groups_along(["z_hi", "z_lo"])
IN_PLANE = groups_along(["y", "x"])


def exchange(pieces, groups):
    return lax.all_to_all(pieces, BOTH, 0, 0, axis_index_groups=groups)


def copies(value, groups):
    return jnp.broadcast_to(value[None], (len(groups[0]),) + value.shape)


def spread(value, groups):
    return exchange(copies(value, groups), groups)


def from_pair(value):
    return lax.all_gather(value, "blk", axis_index_groups=PAIRS, axis=0, tiled=True)


def even_code(points):
    size = jnp.abs(points) * (STEPS / 6.0)
    whole = jnp.floor(size)
    code = jnp.exp2(whole - 14.0) * (1.0 + (size - whole))
    return jnp.where(points < 0.0, -code, code).astype(jnp.float16)


def even_points(code):
    code = code.astype(jnp.float32)
    whole = jnp.floor(jnp.log2(jnp.abs(code)))
    size = (whole + 13.0 + jnp.abs(code) * jnp.exp2(-whole)) * (6.0 / STEPS)
    return jnp.where(code < 0.0, -size, size)


def two_codes(values):
    high = (values.astype(jnp.bfloat16).astype(jnp.float32) * 2.0**13).astype(jnp.float16)
    low = (values - high.astype(jnp.float32) * 2.0**-13) * 2.0**21
    return [high, low.astype(jnp.float16)]


def from_two_codes(high, low):
    return high.astype(jnp.float32) * 2.0**-13 + low.astype(jnp.float32) * 2.0**-21


def parts(value, count):
    found = []
    for _ in range(count):
        part = value.astype(jnp.bfloat16)
        found.append(part)
        value = value - part.astype(jnp.float32)
    return found


def operand(coords, left):
    high, low = parts(coords, 2)
    kept = high.astype(jnp.float32) + low.astype(jnp.float32)
    pieces = parts(jnp.sum(kept * kept, axis=0, keepdims=True), 3)
    ones = [jnp.ones_like(pieces[0])] * 3
    rest = jnp.zeros((DEPTH - 4 * FEAT - 6, coords.shape[1]), jnp.bfloat16)
    if left:
        rows = [high, low, high, low] + pieces + ones
    else:
        high, low = high * -2.0, low * -2.0
        rows = [high, high, low, low] + ones + pieces
    return jnp.concatenate(rows + [rest], axis=0)


def matern(five_dist2):
    five_dist2 = jnp.maximum(five_dist2, 1e-30)
    spread_ = five_dist2 * lax.rsqrt(five_dist2)
    decay = jnp.exp2(spread_ * (-math.log2(math.e)))
    return ((spread_ + 1.0) + five_dist2 * (1.0 / 3.0)) * decay


def ready_kernel(
    points_ref, scales_ref, noise_ref, targets_ref,
    points_out_ref, targets_out_ref, scales_out_ref, noise_out_ref,
):
    points_out_ref[...] = points_ref[...]
    targets_out_ref[...] = targets_ref[...]
    scales_out_ref[...] = jnp.broadcast_to(scales_ref[...].reshape(1, FEAT), (OWN, FEAT)).T
    noise_out_ref[...] = jnp.full((RHS, OWN), noise_ref[0], jnp.float32)


def make_ready(points, length_scales, noise_level, targets):
    vmem = pl.BlockSpec(memory_space=pltpu.VMEM)
    return pl.pallas_call(
        ready_kernel,
        out_shape=(
            pltpu.VMEM((FEAT, OWN), jnp.float32),
            pltpu.VMEM((RHS, OWN), jnp.float32),
            pltpu.VMEM((FEAT, OWN), jnp.float32),
            pltpu.VMEM((RHS, OWN), jnp.float32),
        ),
        in_specs=[vmem, vmem, pl.BlockSpec(memory_space=pltpu.SMEM), vmem],
        out_specs=(vmem, vmem, vmem, vmem),
        name="ready",
    )(points, length_scales, noise_level, targets)


def put_product(total, chunk, product_ref):
    for block in range(WIDE // OWN):
        product_ref[chunk * (WIDE // OWN) + block] = total[:, block * OWN : (block + 1) * OWN]


def probes_of(pieces):
    return jnp.concatenate([piece.astype(jnp.bfloat16) for piece in pieces], axis=1)


def build_kernel(rows_ref, cols_ref, tile_ref, product_ref, left, right, probes, sems, *held):
    for block in range(COLS):
        right[:, block * OWN : (block + 1) * OWN] = operand(cols_ref[block], False)
    for some in range(0, ROWS, 4):
        blocks = [rows_ref[some + i] for i in range(4)]
        at = slice(some * OWN, (some + 4) * OWN)
        scaled = jnp.concatenate([block[:FEAT] for block in blocks], axis=1)
        left[at, :] = operand(scaled, True).T
        probes[:, at] = probes_of([block[FEAT:] for block in blocks])

    def leave(chunk):
        return pltpu.make_async_copy(held[chunk % HELD], tile_ref.at[chunk], sems.at[chunk % HELD])

    def multiply(chunk):
        kernel = held[chunk % HELD][...]
        total = jnp.dot(probes[...], kernel, preferred_element_type=jnp.float32)
        put_product(total, chunk, product_ref)

    for chunk in range(CHUNKS):
        if chunk >= HELD:
            leave(chunk - HELD).wait()
        cols = slice(chunk * WIDE, (chunk + 1) * WIDE)
        dist = jnp.dot(left[...], right[:, cols], preferred_element_type=jnp.float32)
        held[chunk % HELD][...] = matern(dist).astype(jnp.bfloat16)
        if chunk >= 1:
            multiply(chunk - 1)
        leave(chunk).start()
    multiply(CHUNKS - 1)
    for chunk in range(CHUNKS - HELD, CHUNKS):
        leave(chunk).wait()


def build(rows, cols):
    return pl.pallas_call(
        build_kernel,
        out_shape=(
            jax.ShapeDtypeStruct((CHUNKS, ROWS * OWN, WIDE), jnp.bfloat16),
            jax.ShapeDtypeStruct((COLS, RHS, OWN), jnp.float32),
        ),
        in_specs=[pl.BlockSpec(memory_space=pltpu.VMEM)] * 2,
        out_specs=(pl.BlockSpec(memory_space=pl.ANY), pl.BlockSpec(memory_space=pltpu.VMEM)),
        scratch_shapes=[
            pltpu.VMEM((ROWS * OWN, DEPTH), jnp.bfloat16),
            pltpu.VMEM((DEPTH, COLS * OWN), jnp.bfloat16),
            pltpu.VMEM((RHS, ROWS * OWN), jnp.bfloat16),
            pltpu.SemaphoreType.DMA((HELD,)),
            *[pltpu.VMEM((ROWS * OWN, WIDE), jnp.bfloat16) for _ in range(HELD)],
        ],
        compiler_params=pltpu.CompilerParams(vmem_limit_bytes=40 * 2**20),
        name="build",
    )(rows, cols)


def again_kernel(probes_ref, cols_ref, own_ref, tile_ref, product_ref, held, sems):
    def fetch(chunk):
        return pltpu.make_async_copy(tile_ref.at[chunk], held.at[chunk], sems.at[chunk])

    for chunk in range(CHUNKS):
        fetch(chunk).start()
    probes = probes_of([probes_ref[i] for i in range(ROWS)])
    inner = own_ref[...]
    for chunk in range(CHUNKS):
        fetch(chunk).wait()
        total = jnp.dot(probes, held[chunk], preferred_element_type=jnp.float32)
        for part in range(WIDE // OWN):
            block = chunk * (WIDE // OWN) + part
            piece = total[:, part * OWN : (part + 1) * OWN]
            product_ref[block, :RHS] = piece
            inner += piece * cols_ref[block]
    for block in range(COLS):
        product_ref[block, RHS:] = inner


def again(probes, cols, own, tile):
    vmem = pl.BlockSpec(memory_space=pltpu.VMEM)
    return pl.pallas_call(
        again_kernel,
        out_shape=jax.ShapeDtypeStruct((COLS, 2 * RHS, OWN), jnp.float32),
        in_specs=[vmem, vmem, vmem, pl.BlockSpec(memory_space=pl.ANY)],
        out_specs=vmem,
        scratch_shapes=[
            pltpu.VMEM((CHUNKS, ROWS * OWN, WIDE), jnp.bfloat16),
            pltpu.SemaphoreType.DMA((CHUNKS,)),
        ],
        compiler_params=pltpu.CompilerParams(vmem_limit_bytes=40 * 2**20),
        name="again",
    )(probes, cols, own, tile)


def own_sum(partials):
    return jnp.sum(exchange(partials, IN_PLANE), axis=0)


def as_row(sums):
    flat = jnp.stack(sums).reshape(1, -1)
    return jnp.pad(flat, ((0, 0), (0, OWN - flat.shape[1])))


def on_device(points, length_scales, noise_level, targets):
    points, targets, scales, noise = make_ready(points, length_scales, noise_level, targets)
    sent = jnp.concatenate([even_code(points)] + two_codes(targets), axis=0)

    def arrived(blocks):
        coords = even_points(blocks[:, :FEAT]) / scales * SQRT_FIVE
        return coords, from_two_codes(blocks[:, FEAT : FEAT + RHS], blocks[:, FEAT + RHS :])

    rows = jnp.concatenate(arrived(from_pair(spread(sent, ALONG_Z))), axis=1)
    sent, rows = lax.optimization_barrier((sent, rows))
    row_targets = rows[:, FEAT:]
    cols, col_targets = arrived(spread(sent, IN_PLANE))

    tile, partials = build(rows, cols)
    image = own_sum(partials) + noise * targets
    row_image = from_pair(spread(image, ALONG_Z))

    norm = jnp.sum(row_targets * row_targets, axis=(0, 2))
    curve = jnp.sum(row_targets * row_image, axis=(0, 2))
    square = jnp.sum(row_image * row_image, axis=(0, 2))
    sums = jnp.pad(as_row([norm, curve, square]), ((0, 7), (0, 0)))
    plane = spread(jnp.concatenate([image, sums], axis=0), IN_PLANE)
    norm, curve, square = jnp.sum(plane[:, RHS], axis=0)[: 3 * RHS].reshape(3, RHS)
    alpha = norm / curve
    norm_next = norm - 2.0 * alpha * curve + alpha * alpha * square
    ratio = (norm_next / norm)[:, None]
    alpha = alpha[:, None]

    row_direction = (row_targets - alpha * row_image) + ratio * row_targets
    col_direction = (col_targets - alpha * plane[:, :RHS]) + ratio * col_targets
    residual = targets - alpha * image
    direction = residual + ratio * targets
    noisy = noise * direction
    both = own_sum(again(row_direction, col_direction, noisy * direction, tile))
    image_next = both[:RHS] + noisy
    inner = as_row([jnp.sum(both[RHS:], axis=1)])
    curve_next = jnp.sum(from_pair(spread(inner, ALONG_Z)), axis=0)[0, :RHS]
    alpha_next = (norm_next / curve_next)[:, None]
    solution_field = alpha * targets + alpha_next * direction
    residual = residual - alpha_next * image_next
    return (solution_field, residual)


def solution(mesh):
    return jax.shard_map(
        on_device,
        mesh=mesh,
        in_specs=(P(None, BOTH), P(), P(), P(None, BOTH)),
        out_specs=(P(None, BOTH), P(None, BOTH)),
        check_vma=False,
    )
```

```python
import itertools
import math

import jax
import jax.numpy as jnp
from jax import lax
from jax.experimental import pallas as pl
from jax.experimental.pallas import tpu as pltpu
from jax.sharding import PartitionSpec as P

FEAT = 32
RHS = 16
OWN = 128
ROWS = 32
COLS = 16
DEPTH = 144
WIDE = 256
CHUNKS = COLS * OWN // WIDE
STEPS = 29.9
SQRT_FIVE = math.sqrt(5.0)
HELD = 4

BOTH = ("grp", "blk")
SIZES = {"x": 4, "z_lo": 4, "y": 4, "z_hi": 4, "core": 2}
PAIRS = [[2 * i, 2 * i + 1] for i in range(16)]


def groups_along(axes):
    rest = [axis for axis in SIZES if axis not in axes]
    found = []
    for fixed in itertools.product(*[range(SIZES[axis]) for axis in rest]):
        members = []
        for moving in itertools.product(*[range(SIZES[axis]) for axis in axes]):
            place = dict(zip(rest, fixed)) | dict(zip(axes, moving))
            index = 0
            for axis in SIZES:
                index = index * SIZES[axis] + place[axis]
            members.append(index)
        found.append(members)
    return found


ALONG_Z = groups_along(["z_hi", "z_lo"])
IN_PLANE = groups_along(["y", "x"])


def exchange(pieces, groups):
    return lax.all_to_all(pieces, BOTH, 0, 0, axis_index_groups=groups)


def copies(value, groups):
    return jnp.broadcast_to(value[None], (len(groups[0]),) + value.shape)


def spread(value, groups):
    return exchange(copies(value, groups), groups)


def from_pair(value):
    return lax.all_gather(value, "blk", axis_index_groups=PAIRS, axis=0, tiled=True)


def even_code(points):
    size = jnp.abs(points) * (STEPS / 6.0)
    whole = jnp.floor(size)
    code = jnp.exp2(whole - 14.0) * (1.0 + (size - whole))
    return jnp.where(points < 0.0, -code, code).astype(jnp.float16)


def even_points(code):
    code = code.astype(jnp.float32)
    whole = jnp.floor(jnp.log2(jnp.abs(code)))
    size = (whole + 13.0 + jnp.abs(code) * jnp.exp2(-whole)) * (6.0 / STEPS)
    return jnp.where(code < 0.0, -size, size)


def two_codes(values):
    high = (values.astype(jnp.bfloat16).astype(jnp.float32) * 2.0**13).astype(jnp.float16)
    low = (values - high.astype(jnp.float32) * 2.0**-13) * 2.0**21
    return [high, low.astype(jnp.float16)]


def from_two_codes(high, low):
    return high.astype(jnp.float32) * 2.0**-13 + low.astype(jnp.float32) * 2.0**-21


def parts(value, count):
    found = []
    for _ in range(count):
        part = value.astype(jnp.bfloat16)
        found.append(part)
        value = value - part.astype(jnp.float32)
    return found


def operand(coords, left):
    high, low = parts(coords, 2)
    kept = high.astype(jnp.float32) + low.astype(jnp.float32)
    pieces = parts(jnp.sum(kept * kept, axis=0, keepdims=True), 3)
    ones = [jnp.ones_like(pieces[0])] * 3
    rest = jnp.zeros((DEPTH - 4 * FEAT - 6, coords.shape[1]), jnp.bfloat16)
    if left:
        rows = [high, low, high, low] + pieces + ones
    else:
        high, low = high * -2.0, low * -2.0
        rows = [high, high, low, low] + ones + pieces
    return jnp.concatenate(rows + [rest], axis=0)


def matern(five_dist2):
    five_dist2 = jnp.maximum(five_dist2, 1e-30)
    spread_ = five_dist2 * lax.rsqrt(five_dist2)
    decay = jnp.exp2(spread_ * (-math.log2(math.e)))
    return ((spread_ + 1.0) + five_dist2 * (1.0 / 3.0)) * decay


def ready_kernel(
    points_ref, scales_ref, noise_ref, targets_ref,
    points_out_ref, targets_out_ref, scales_out_ref, noise_out_ref,
):
    points_out_ref[...] = points_ref[...]
    targets_out_ref[...] = targets_ref[...]
    scales_out_ref[...] = jnp.broadcast_to(scales_ref[...].reshape(1, FEAT), (OWN, FEAT)).T
    noise_out_ref[...] = jnp.full((RHS, OWN), noise_ref[0], jnp.float32)


def make_ready(points, length_scales, noise_level, targets):
    vmem = pl.BlockSpec(memory_space=pltpu.VMEM)
    return pl.pallas_call(
        ready_kernel,
        out_shape=(
            pltpu.VMEM((FEAT, OWN), jnp.float32),
            pltpu.VMEM((RHS, OWN), jnp.float32),
            pltpu.VMEM((FEAT, OWN), jnp.float32),
            pltpu.VMEM((RHS, OWN), jnp.float32),
        ),
        in_specs=[vmem, vmem, pl.BlockSpec(memory_space=pltpu.SMEM), vmem],
        out_specs=(vmem, vmem, vmem, vmem),
        name="ready",
    )(points, length_scales, noise_level, targets)


def put_product(total, chunk, product_ref):
    for block in range(WIDE // OWN):
        product_ref[chunk * (WIDE // OWN) + block] = total[:, block * OWN : (block + 1) * OWN]


def probes_of(pieces):
    return jnp.concatenate([piece.astype(jnp.bfloat16) for piece in pieces], axis=1)


def build_kernel(rows_ref, cols_ref, tile_ref, kept_ref, product_ref, left, right, probes, sems, *held):
    for block in range(COLS):
        right[:, block * OWN : (block + 1) * OWN] = operand(cols_ref[block], False)
    for some in range(0, ROWS, 4):
        blocks = [rows_ref[some + i] for i in range(4)]
        at = slice(some * OWN, (some + 4) * OWN)
        scaled = jnp.concatenate([block[:FEAT] for block in blocks], axis=1)
        left[at, :] = operand(scaled, True).T
        probes[:, at] = probes_of([block[FEAT:] for block in blocks])

    def leave(chunk):
        return pltpu.make_async_copy(held[chunk % HELD], tile_ref.at[chunk], sems.at[chunk % HELD])

    def place(chunk):
        return kept_ref if chunk == CHUNKS - 1 else held[chunk % HELD]

    def multiply(chunk):
        kernel = place(chunk)[...]
        total = jnp.dot(probes[...], kernel, preferred_element_type=jnp.float32)
        put_product(total, chunk, product_ref)

    for chunk in range(CHUNKS):
        if HELD <= chunk < CHUNKS - 1:
            leave(chunk - HELD).wait()
        cols = slice(chunk * WIDE, (chunk + 1) * WIDE)
        dist = jnp.dot(left[...], right[:, cols], preferred_element_type=jnp.float32)
        place(chunk)[...] = matern(dist).astype(jnp.bfloat16)
        if chunk >= 1:
            multiply(chunk - 1)
        if chunk < CHUNKS - 1:
            leave(chunk).start()
    multiply(CHUNKS - 1)
    for chunk in range(CHUNKS - 1 - HELD, CHUNKS - 1):
        leave(chunk).wait()


def build(rows, cols):
    return pl.pallas_call(
        build_kernel,
        out_shape=(
            jax.ShapeDtypeStruct((CHUNKS - 1, ROWS * OWN, WIDE), jnp.bfloat16),
            pltpu.VMEM((ROWS * OWN, WIDE), jnp.bfloat16),
            jax.ShapeDtypeStruct((COLS, RHS, OWN), jnp.float32),
        ),
        in_specs=[pl.BlockSpec(memory_space=pltpu.VMEM)] * 2,
        out_specs=(
            pl.BlockSpec(memory_space=pl.ANY),
            pl.BlockSpec(memory_space=pltpu.VMEM),
            pl.BlockSpec(memory_space=pltpu.VMEM),
        ),
        scratch_shapes=[
            pltpu.VMEM((ROWS * OWN, DEPTH), jnp.bfloat16),
            pltpu.VMEM((DEPTH, COLS * OWN), jnp.bfloat16),
            pltpu.VMEM((RHS, ROWS * OWN), jnp.bfloat16),
            pltpu.SemaphoreType.DMA((HELD,)),
            *[pltpu.VMEM((ROWS * OWN, WIDE), jnp.bfloat16) for _ in range(HELD)],
        ],
        compiler_params=pltpu.CompilerParams(vmem_limit_bytes=40 * 2**20),
        name="build",
    )(rows, cols)


def again_kernel(probes_ref, cols_ref, own_ref, tile_ref, kept_ref, product_ref, held, sems):
    def fetch(chunk):
        return pltpu.make_async_copy(tile_ref.at[chunk], held.at[chunk], sems.at[chunk])

    for chunk in range(CHUNKS - 1):
        fetch(chunk).start()
    probes = probes_of([probes_ref[i] for i in range(ROWS)])
    inner = own_ref[...]
    for chunk in [CHUNKS - 1, *range(CHUNKS - 1)]:
        if chunk < CHUNKS - 1:
            fetch(chunk).wait()
        kernel = kept_ref[...] if chunk == CHUNKS - 1 else held[chunk]
        total = jnp.dot(probes, kernel, preferred_element_type=jnp.float32)
        for part in range(WIDE // OWN):
            block = chunk * (WIDE // OWN) + part
            piece = total[:, part * OWN : (part + 1) * OWN]
            product_ref[block, :RHS] = piece
            inner += piece * cols_ref[block]
    for block in range(COLS):
        product_ref[block, RHS:] = inner


def again(probes, cols, own, tile, kept):
    vmem = pl.BlockSpec(memory_space=pltpu.VMEM)
    return pl.pallas_call(
        again_kernel,
        out_shape=jax.ShapeDtypeStruct((COLS, 2 * RHS, OWN), jnp.float32),
        in_specs=[vmem, vmem, vmem, pl.BlockSpec(memory_space=pl.ANY), vmem],
        out_specs=vmem,
        scratch_shapes=[
            pltpu.VMEM((CHUNKS - 1, ROWS * OWN, WIDE), jnp.bfloat16),
            pltpu.SemaphoreType.DMA((CHUNKS - 1,)),
        ],
        compiler_params=pltpu.CompilerParams(vmem_limit_bytes=40 * 2**20),
        name="again",
    )(probes, cols, own, tile, pltpu.with_memory_space_constraint(kept, pltpu.VMEM))


def own_sum(partials):
    return jnp.sum(exchange(partials, IN_PLANE), axis=0)


def as_row(sums):
    flat = jnp.stack(sums).reshape(1, -1)
    return jnp.pad(flat, ((0, 0), (0, OWN - flat.shape[1])))


def on_device(points, length_scales, noise_level, targets):
    points, targets, scales, noise = make_ready(points, length_scales, noise_level, targets)
    sent = jnp.concatenate([even_code(points)] + two_codes(targets), axis=0)

    def arrived(blocks):
        coords = even_points(blocks[:, :FEAT]) / scales * SQRT_FIVE
        return coords, from_two_codes(blocks[:, FEAT : FEAT + RHS], blocks[:, FEAT + RHS :])

    rows = jnp.concatenate(arrived(from_pair(spread(sent, ALONG_Z))), axis=1)
    sent, rows = lax.optimization_barrier((sent, rows))
    row_targets = rows[:, FEAT:]
    cols, col_targets = arrived(spread(sent, IN_PLANE))

    tile, kept, partials = build(rows, cols)
    image = own_sum(partials) + noise * targets
    row_image = from_pair(spread(image, ALONG_Z))

    norm = jnp.sum(row_targets * row_targets, axis=(0, 2))
    curve = jnp.sum(row_targets * row_image, axis=(0, 2))
    square = jnp.sum(row_image * row_image, axis=(0, 2))
    sums = jnp.pad(as_row([norm, curve, square]), ((0, 7), (0, 0)))
    plane = spread(jnp.concatenate([image, sums], axis=0), IN_PLANE)
    norm, curve, square = jnp.sum(plane[:, RHS], axis=0)[: 3 * RHS].reshape(3, RHS)
    alpha = norm / curve
    norm_next = norm - 2.0 * alpha * curve + alpha * alpha * square
    ratio = (norm_next / norm)[:, None]
    alpha = alpha[:, None]

    row_direction = (row_targets - alpha * row_image) + ratio * row_targets
    col_direction = (col_targets - alpha * plane[:, :RHS]) + ratio * col_targets
    residual = targets - alpha * image
    direction = residual + ratio * targets
    noisy = noise * direction
    both = own_sum(again(row_direction, col_direction, noisy * direction, tile, kept))
    image_next = both[:RHS] + noisy
    inner = as_row([jnp.sum(both[RHS:], axis=1)])
    curve_next = jnp.sum(from_pair(spread(inner, ALONG_Z)), axis=0)[0, :RHS]
    alpha_next = (norm_next / curve_next)[:, None]
    solution_field = alpha * targets + alpha_next * direction
    residual = residual - alpha_next * image_next
    return (solution_field, residual)


def solution(mesh):
    return jax.shard_map(
        on_device,
        mesh=mesh,
        in_specs=(P(None, BOTH), P(), P(), P(None, BOTH)),
        out_specs=(P(None, BOTH), P(None, BOTH)),
        check_vma=False,
    )
```
